32 devices in a mesh: gx: 4 (over y, x), gy: 8 (over z, core).
Axes of the slice: x: 2, y: 2, z: 4, core: 2. Of those that a mesh axis runs over, the one named last changes fastest.
Arguments:
- weights: float32 [4, 8, 64, 32, 128], P('gx', 'gy'), may hold values from -6 to 6
- coef_first: float32 [8, 6, 64], P('gy'), may hold values from 0.25 to 1
- coef_second: float32 [14, 64], replicated, may hold values from 0.25 to 1
Outputs:
- final_weights: float32 [8, 256, 32, 128], P('gy', 'gx')
The draws below stay inside these ranges and needn't reach their ends.
All inputs are finite; a program needn't handle non-finite values.
Results may differ from the reference program's by a relative error of at most 0.0003.
Values sent between devices are 32-bit elements; how exact they have to be, the bound alone decides.
A program may use at most 64 MiB of HBM per device.

```python
import math
import jax
import jax.numpy as jnp
import numpy as np
from jax import lax

N = 4096
MX = 64
MY = 32
XLEVELS = 2
YLEVELS = 3
XTAB = 6
YTAB = 14
N_GX = 4
N_GY = 8


def block_levels(own_key, dims, shards, low, largest):
    level = 1.0
    for axis_at, blocks in shards:
        heights = jax.random.uniform(jax.random.fold_in(jax.random.fold_in(own_key, 6), axis_at), (blocks,), jnp.float32, low / len(shards), largest / len(shards))
        level = level * jnp.repeat(jnp.exp(heights), dims[axis_at] // blocks).reshape((-1,) + (1,) * (len(dims) - 1 - axis_at))
    return level


def normal_values(stream_key, dims, deviation, bound, cuts=(), held_as=jnp.bfloat16):
    gain = block_levels(stream_key, dims, cuts, -0.22, 0.18) if cuts else 1.0
    entries = jax.random.normal(stream_key, dims, jnp.float32) * deviation * gain
    return jnp.minimum(jnp.maximum(entries, -bound), bound).astype(held_as)


def setup_inputs(seed: int = 0) -> dict:
    streams_of = jax.random.split(jax.random.key(seed), 4)
    return {
        "weights": normal_values(streams_of[0], (N_GX, N_GY, MX, MY, 128), 1.0, 6.0, ((0, 4), (1, 8)), jnp.float32),
        "coef_first": jnp.clip(0.25 + 0.75 * jax.random.uniform(streams_of[1], (N_GY, XTAB, 64), jnp.float32) ** block_levels(streams_of[1], (N_GY, XTAB, 64), ((0, 8),), -0.2, 0.2), 0.25, 1.0),
        "coef_second": jnp.clip(jax.random.uniform(streams_of[2], (YTAB, 64), jnp.float32, 0.25, 1.0), 0.25, 1.0),
    }


TWO_PI = 2.0 * math.pi

def cheb_nodes():
    return np.cos(np.pi * (2.0 * np.arange(8) + 1.0) / 16.0)

def lagrange_child(child_half):
    nodes = cheb_nodes()
    targets = (2.0 * child_half - 1.0) / 2.0 + nodes / 2.0
    result = np.ones((8, 8))
    for target in range(8):
        for factor in range(8):
            if factor != target:
                result[target, :] = result[target, :] * (targets - nodes[factor]) / (nodes[target] - nodes[factor])
    return result

def kron_stack(along_second):
    matrices = []
    for child_half in range(2):
        lagrange = lagrange_child(child_half)
        if along_second:
            middle = np.kron(np.eye(8), lagrange)
        else:
            middle = np.kron(lagrange, np.eye(8))
        matrices.append(np.kron(np.eye(2), middle).T)
    return jnp.asarray(np.stack(matrices), dtype=jnp.float32)

def node_pattern(along_second):
    nodes = cheb_nodes()
    if along_second:
        layout = np.tile(nodes, 8)
    else:
        layout = np.repeat(nodes, 8)
    return jnp.asarray(layout, dtype=jnp.float32)

def rotate_apply(values, phases, kernel):
    angles = phases * TWO_PI
    cosine = jnp.cos(angles)
    sines = jnp.sin(angles)
    real_part = values[..., :64]
    imag_part = values[..., 64:]
    rotated = jnp.concatenate([cosine * real_part - sines * imag_part, sines * real_part + cosine * imag_part], axis=-1)
    mapped = jnp.dot(rotated.reshape(-1, 128), kernel, precision=lax.Precision.HIGHEST, preferred_element_type=jnp.float32)
    return mapped.reshape(values.shape)

def bend_factor(centre, across, offset):
    shifted = centre - offset
    return offset * (centre + shifted) / (jnp.sqrt(centre * centre + across * across) + jnp.sqrt(shifted * shifted + across * across))

def x_level(current, coef_rows, level_num, m_start, n_gx):
    halves = current.shape[0] // 2
    freq_boxes = current.shape[1]
    columns = current.shape[2]
    box_width = N / (MX * 2 ** level_num)
    kernels = kron_stack(False)
    pattern = node_pattern(False)
    centre = ((m_start + jnp.arange(freq_boxes)).astype(jnp.float32) + 0.5) * box_width - N / 2
    across = (jnp.arange(columns).astype(jnp.float32) + 0.5) * (N / MY) - N / 2
    results = []
    for pick_half in range(2):
        offset = box_width / 4 * (1 - 2 * pick_half)
        bending = bend_factor(centre[:, None], across[None, :], offset)
        summed = None
        for child_half in range(2):
            box_index = (jnp.arange(halves) * 2 + child_half).astype(jnp.float32)
            location = (box_index[:, None] + 0.5 + 0.5 * pattern[None, :]) * (2 ** level_num / n_gx)
            phases = location[:, None, None, :] * offset + coef_rows[child_half::2][:, None, None, :] * bending[None, :, :, None]
            contrib = rotate_apply(current[child_half::2], phases, kernels[child_half])
            summed = contrib if summed is None else summed + contrib
        results.append(summed)
    return jnp.stack(results, axis=2).reshape(halves, freq_boxes * 2, columns, 128)

def y_level(current, coef_rows, level_num, m_start, n_gy, n_gx):
    halves = current.shape[0] // 2
    row_count = current.shape[1]
    freq_boxes = current.shape[2]
    box_width = N / (MY * 2 ** level_num)
    kernels = kron_stack(True)
    pattern = node_pattern(True)
    leading = ((m_start + jnp.arange(row_count)).astype(jnp.float32) + 0.5) * (N / (MX * n_gx)) - N / 2
    centre = (jnp.arange(freq_boxes).astype(jnp.float32) + 0.5) * box_width - N / 2
    results = []
    for pick_half in range(2):
        offset = box_width / 4 * (1 - 2 * pick_half)
        bending = bend_factor(centre[None, :], leading[:, None], offset)
        summed = None
        for child_half in range(2):
            box_index = (jnp.arange(halves) * 2 + child_half).astype(jnp.float32)
            location = (box_index[:, None] + 0.5 + 0.5 * pattern[None, :]) * (2 ** level_num / n_gy)
            phases = location[:, None, None, :] * offset + coef_rows[child_half::2][:, None, None, :] * bending[None, :, :, None]
            contrib = rotate_apply(current[child_half::2], phases, kernels[child_half])
            summed = contrib if summed is None else summed + contrib
        results.append(summed)
    return jnp.stack(results, axis=3).reshape(halves, row_count, freq_boxes * 2, 128)

def reversed_order(count, bit_count):
    return np.array([sum(((value >> shift & 1) << bit_count - 1 - shift for shift in range(bit_count))) for value in range(count)], dtype=np.int32)

def reference(weights, coef_first, coef_second):

    def x_section(operands):
        current, table_rows = operands
        for level_num in range(XLEVELS):
            start_row = sum((N_GX >> shift for shift in range(level_num)))
            current = x_level(current, table_rows[start_row:start_row + (N_GX >> level_num)], level_num, 0, N_GX)
        return current[0]
    mixed = lax.map(x_section, (jnp.moveaxis(weights, 1, 0), coef_first))
    blocks = mixed.reshape(N_GY, N_GX, MX, MY, 128).transpose(1, 0, 2, 3, 4)

    def y_section(operands):
        current, m_start = operands
        for level_num in range(YLEVELS):
            start_row = sum((N_GY >> shift for shift in range(level_num)))
            current = y_level(current, coef_second[start_row:start_row + (N_GY >> level_num)], level_num, m_start, N_GY, N_GX)
        return current[0]
    starts = jnp.arange(N_GX, dtype=jnp.int32) * MX
    finished = lax.map(y_section, (blocks, starts))
    finished = finished.reshape(N_GX * MX, MY, N_GY, 128)
    picked = finished[:, :, reversed_order(N_GY, YLEVELS), :]
    return jnp.transpose(picked, (2, 0, 1, 3))
```

```python
import functools
import math

import jax
import jax.numpy as jnp
import numpy as np
from jax import lax
from jax.experimental import pallas as pl
from jax.experimental.pallas import tpu as pltpu
from jax.sharding import PartitionSpec as P

N = 4096
MX = 64
MY = 32


TWO_PI = 2.0 * math.pi


def from_partner(value, axis, apart):
    mask = 2**apart
    pairs = [(source, source ^ mask) for source in range(lax.axis_size(axis))]
    return lax.ppermute(value, axis, pairs)


def cheb_nodes():
    return np.cos(np.pi * (2.0 * np.arange(8) + 1.0) / 16.0)


def lagrange_child(child_half):
    nodes = cheb_nodes()
    targets = (2.0 * child_half - 1.0) / 2.0 + nodes / 2.0
    result = np.ones((8, 8))
    for target in range(8):
        for factor in range(8):
            if factor != target:
                result[target, :] = (
                    result[target, :] * (targets - nodes[factor]) / (nodes[target] - nodes[factor])
                )
    return result


def kron_stack(along_second):
    matrices = []
    for child_half in range(2):
        lagrange = lagrange_child(child_half)
        if along_second:
            middle = np.kron(np.eye(8), lagrange)
        else:
            middle = np.kron(lagrange, np.eye(8))
        matrices.append(np.kron(np.eye(2), middle).T)
    return jnp.asarray(np.stack(matrices), dtype=jnp.float32)


def node_pattern(along_second):
    nodes = cheb_nodes()
    if along_second:
        layout = np.tile(nodes, 8)
    else:
        layout = np.repeat(nodes, 8)
    return jnp.asarray(layout, dtype=jnp.float32)


def rotate_apply(values, phases, kernel):
    angles = phases * TWO_PI
    cosine = jnp.cos(angles)
    sines = jnp.sin(angles)
    real_part = values[..., :64]
    imag_part = values[..., 64:]
    rotated = jnp.concatenate(
        [cosine * real_part - sines * imag_part, sines * real_part + cosine * imag_part], axis=-1
    )
    mapped = jnp.dot(
        rotated.reshape(-1, 128),
        kernel,
        precision=lax.Precision.HIGHEST,
        preferred_element_type=jnp.float32,
    )
    return mapped.reshape(values.shape)


def bend_factor(centre, across, offset):
    shifted = centre - offset
    return (
        offset
        * (centre + shifted)
        / (
            jnp.sqrt(centre * centre + across * across)
            + jnp.sqrt(shifted * shifted + across * across)
        )
    )


def path_bits(device_pos, level_num):
    result = jnp.int32(0)
    for shift in range(level_num):
        result = result + ((device_pos >> shift & 1) << level_num - 1 - shift)
    return result


def x_term(current, table_rows, level_num, path_value, box_pos, pick_half, n_gx):
    freq_boxes = current.shape[0]
    columns = current.shape[1]
    box_width = N / (MX * 2**level_num)
    kernels = kron_stack(False)
    pattern = node_pattern(False)
    centre = (
        (jnp.arange(freq_boxes) * 2**level_num + path_value).astype(jnp.float32) + 0.5
    ) * box_width - N / 2
    across = (jnp.arange(columns).astype(jnp.float32) + 0.5) * (N / MY) - N / 2
    offset = box_width / 4 * (1 - 2 * pick_half).astype(jnp.float32)
    bending = bend_factor(centre[:, None], across[None, :], offset)
    location = (box_pos.astype(jnp.float32) + 0.5 + 0.5 * pattern) * (2**level_num / n_gx)
    start_row = sum((n_gx >> shift for shift in range(level_num)))
    coef_row = lax.dynamic_index_in_dim(table_rows, start_row + box_pos, 0, keepdims=False)
    phases = location[None, None, :] * offset + coef_row[None, None, :] * bending[:, :, None]
    return rotate_apply(current, phases, kernels[box_pos % 2])


def y_term(current, table_rows, level_num, path_value, box_pos, pick_half, n_gy, m_start, n_gx):
    row_count = current.shape[0]
    freq_boxes = current.shape[1]
    box_width = N / (MY * 2**level_num)
    kernels = kron_stack(True)
    pattern = node_pattern(True)
    leading = ((m_start + jnp.arange(row_count)).astype(jnp.float32) + 0.5) * (
        N / (MX * n_gx)
    ) - N / 2
    centre = (
        (jnp.arange(freq_boxes) * 2**level_num + path_value).astype(jnp.float32) + 0.5
    ) * box_width - N / 2
    offset = box_width / 4 * (1 - 2 * pick_half).astype(jnp.float32)
    bending = bend_factor(centre[None, :], leading[:, None], offset)
    location = (box_pos.astype(jnp.float32) + 0.5 + 0.5 * pattern) * (2**level_num / n_gy)
    start_row = sum((n_gy >> shift for shift in range(level_num)))
    coef_row = lax.dynamic_index_in_dim(table_rows, start_row + box_pos, 0, keepdims=False)
    phases = location[None, None, :] * offset + coef_row[None, None, :] * bending[:, :, None]
    return rotate_apply(current, phases, kernels[box_pos % 2])


def on_device(weights, coef_first, coef_second):
    n_gx = lax.axis_size("gx")
    n_gy = lax.axis_size("gy")
    x_bits = n_gx.bit_length() - 1
    y_bits = n_gy.bit_length() - 1
    gx_index = lax.axis_index("gx")
    gy_index = lax.axis_index("gy")
    table_first = coef_first[0]
    current = weights[0, 0]
    per_block = MX // n_gx
    for level_num in range(x_bits):
        box_pos = gx_index >> level_num
        own_half = box_pos % 2
        path_value = path_bits(gx_index, level_num)
        partner = from_partner(current, "gx", level_num)
        current = x_term(
            current, table_first, level_num, path_value, box_pos, own_half, n_gx
        ) + x_term(partner, table_first, level_num, path_value, box_pos ^ 1, own_half, n_gx)
    blocks = current.reshape(n_gx, per_block, MY, 128)
    gathered = lax.all_to_all(blocks, "gx", split_axis=0, concat_axis=0, tiled=True)
    gathered = gathered.reshape((2,) * x_bits + (per_block, MY, 128))
    gathered = jnp.transpose(
        gathered, tuple(reversed(range(x_bits))) + tuple(range(x_bits, x_bits + 3))
    )
    gathered = gathered.reshape(n_gx, per_block, MY, 128)
    current = jnp.transpose(gathered, (1, 0, 2, 3)).reshape(MX, MY, 128)
    m_start = gx_index * MX
    for level_num in range(y_bits):
        box_pos = gy_index >> level_num
        own_half = box_pos % 2
        path_value = path_bits(gy_index, level_num)
        partner = from_partner(current, "gy", level_num)
        current = y_term(
            current, coef_second, level_num, path_value, box_pos, own_half, n_gy, m_start, n_gx
        ) + y_term(
            partner, coef_second, level_num, path_value, box_pos ^ 1, own_half, n_gy, m_start, n_gx
        )
    return current[None]


LANES = 128
MESH = pl.DeviceIdType.MESH


def blocks_fit(n_gx, n_gy):
    per_gx = MX // n_gx
    if MX % n_gx or (per_gx * MY) % LANES or LANES % MY or n_gy % n_gx:
        return False
    return (per_gx * MY // LANES) % (n_gy // n_gx) == 0


def chebyshev_fit(func, degree):
    grid = 0.25 * (1 + np.cos(np.pi * (np.arange(400) + 0.5) / 400)) * 0.5
    series = np.polynomial.chebyshev.Chebyshev.fit(grid, func(grid), degree, domain=[0.0, 0.25])
    return [float(c) for c in series.convert(kind=np.polynomial.Polynomial).coef]


def horner(coefs, arg):
    result = coefs[-1]
    for coef in coefs[-2::-1]:
        result = result * arg + coef
    return result


COS_FIT = chebyshev_fit(lambda t: np.cos(np.pi * np.sqrt(t)), 5)
SIN_FIT = chebyshev_fit(lambda t: 2.0 * np.sinc(np.sqrt(t)) * np.pi, 5)
ROUNDER = 1.5 * 2.0**23


def cos_sin_turns(turns):
    part = turns - ((turns + ROUNDER) - ROUNDER)
    square = part * part
    cos_half = horner(COS_FIT, square)
    twice_sin_half = horner(SIN_FIT, square) * part
    return 1.0 - 0.5 * (twice_sin_half * twice_sin_half), twice_sin_half * cos_half


def merge(load, coef, bending, scale, box, store):
    nodes = cheb_nodes()
    lagrange = lagrange_child(0)
    plus = [[None] * 4, [None] * 4]
    minus = [[None] * 4, [None] * 4]
    bases = [scale * (2 * box + c + 0.5) for c in range(2)]
    for s in range(8):
        rotated = []
        for c in range(2):
            at = s if c == 0 else 7 - s
            turns = coef(c, at) * bending + (bases[c] + scale * float(0.5 * nodes[at]))
            cosine, sine = cos_sin_turns(turns)
            real, imag = load(c, 0, at), load(c, 1, at)
            rotated.append((cosine * real - sine * imag, sine * real + cosine * imag))
        for r in range(2):
            total = rotated[0][r] + rotated[1][r]
            apart = rotated[0][r] - rotated[1][r]
            for a in range(4):
                even = total * float(0.5 * (lagrange[a, s] + lagrange[7 - a, s]))
                odd = apart * float(0.5 * (lagrange[a, s] - lagrange[7 - a, s]))
                plus[r][a] = even if s == 0 else plus[r][a] + even
                minus[r][a] = odd if s == 0 else minus[r][a] + odd
    for r in range(2):
        for a in range(4):
            store(r, a, plus[r][a] + minus[r][a])
            store(r, 7 - a, plus[r][a] - minus[r][a])


def wait_bytes(ref, sem):
    pltpu.make_async_copy(ref, ref, sem).wait()


def butterfly_kernel(
    n_gx, n_gy, w_ref, cf_ref, cs_ref, o_ref,
    x_in, x_a, x_b, x_out, y_in, y_a, y_b, y_t, y_out, cx, cy,
    send_a, recv_a, send_b, recv_b, send_c, recv_c,
):
    gx = lax.axis_index("gx")
    gy = lax.axis_index("gy")
    x_bits = n_gx.bit_length() - 1
    y_bits = n_gy.bit_length() - 1
    per_gx = MX // n_gx
    rows = LANES // MY
    n_lb = per_gx // rows
    fan = n_gy // n_gx
    n_slot = n_lb // fan

    barrier = pltpu.get_barrier_semaphore()
    for step in range(1, n_gx):
        pl.semaphore_signal(
            barrier, inc=1, device_id=((gx + step) % n_gx, gy), device_id_type=MESH
        )
    for step in range(1, n_gy):
        pl.semaphore_signal(
            barrier, inc=1, device_id=(gx, (gy + step) % n_gy), device_id_type=MESH
        )
    pl.semaphore_wait(barrier, n_gx + n_gy - 2)

    def first_copy(lb, step):
        peer = (gx + step) % n_gx
        return pltpu.make_async_remote_copy(
            src_ref=w_ref.at[peer * n_lb + lb],
            dst_ref=x_in.at[gx, lb],
            send_sem=send_a.at[lb, step],
            recv_sem=recv_a.at[lb, gx],
            device_id=(peer, gy),
            device_id_type=MESH,
        )

    for lb in range(n_lb):
        for step in range(1, n_gx):
            first_copy(lb, step).start()
        pltpu.make_async_copy(
            w_ref.at[gx * n_lb + lb], x_in.at[gx, lb], recv_a.at[lb, gx]
        ).start()

    for source, spread in ((cf_ref, cx), (cs_ref, cy)):
        for row in range(source.shape[0]):
            line = jnp.broadcast_to(source[row : row + 1, :], (LANES, 64))
            spread[row] = line.T

    lane = lax.broadcasted_iota(jnp.int32, (8, LANES), 1)
    lane_m = lane // MY
    lane_b = lane % MY
    second = (lane_b.astype(jnp.float32) + 0.5) * (N / MY) - N / 2

    def first_block(lb):
        return gx * per_gx + lb * rows + lane_m

    def second_peer(lb, step):
        return (gy // fan + step) % n_gx * fan + lb % fan

    def second_copy(lb, peer, gets_local):
        z = peer // fan
        slot = lb // fan
        if gets_local:
            return pltpu.make_async_copy(
                x_out.at[lb, z], y_in.at[slot, gy], recv_b.at[slot, gy]
            )
        return pltpu.make_async_remote_copy(
            src_ref=x_out.at[lb, z],
            dst_ref=y_in.at[slot, gy],
            send_sem=send_b.at[lb, z],
            recv_sem=recv_b.at[slot, gy],
            device_id=(gx, peer),
            device_id_type=MESH,
        )

    def x_block(lb, carry):
        for i in range(n_gx):
            wait_bytes(x_in.at[i, lb], recv_a.at[lb, i])

        def turn(i, carry):
            x_a[i] = x_in[i, lb].T
            return carry

        lax.fori_loop(0, n_gx, turn, 0)
        held, other = x_a, x_b
        for level in range(x_bits):
            halves = n_gx >> level + 1
            width = N / (MX * 2**level)
            start = sum(n_gx >> k for k in range(level))
            last = level == x_bits - 1
            target = x_out.at[lb] if last else other

            def unit(u, carry, held=held, target=target, halves=halves, width=width,
                     start=start, level=level):
                box = u % halves
                path = u // halves
                sign = (1 - 2 * (path % 2)).astype(jnp.float32)
                centre = (
                    (first_block(lb) * 2**level + path // 2).astype(jnp.float32) + 0.5
                ) * width - N / 2
                bending = bend_factor(centre, second, sign * (width / 4))
                at = path // 2 * (2 * halves) + 2 * box

                def load(c, r, s):
                    return held[at + c, r * 64 + s * 8 : r * 64 + s * 8 + 8, :]

                def coef(c, s):
                    return cx[start + 2 * box + c, s * 8 : s * 8 + 8, :]

                def store(r, a, value):
                    target[u, r * 64 + a * 8 : r * 64 + a * 8 + 8, :] = value

                scale = sign * (width / 4 * 2**level / n_gx)
                merge(load, coef, bending, scale, box.astype(jnp.float32), store)
                return carry

            lax.fori_loop(0, n_gx, unit, 0)
            held, other = target, held

        def send(step, carry):
            peer = second_peer(lb, step + n_gx // 2)

            @pl.when(peer == gy)
            def _():
                second_copy(lb, peer, True).start()

            @pl.when(peer != gy)
            def _():
                second_copy(lb, peer, False).start()

            return carry

        lax.fori_loop(0, n_gx, send, 0)
        return carry

    lax.fori_loop(0, n_lb, x_block, 0)

    def reverse(value):
        result = 0
        for shift in range(y_bits):
            result = result * 2 + value // 2**shift % 2
        return result

    def third_copy(slot, peer, gets_local):
        here = slot * fan + gy % fan
        place = o_ref.at[here, :, gy // fan]
        if gets_local:
            return pltpu.make_async_copy(y_out.at[slot, peer], place, recv_c.at[slot, gy])
        return pltpu.make_async_remote_copy(
            src_ref=y_out.at[slot, peer],
            dst_ref=place,
            send_sem=send_c.at[slot, peer],
            recv_sem=recv_c.at[slot, gy],
            device_id=(gx, peer),
            device_id_type=MESH,
        )

    def y_block(slot, carry):
        lb = slot * fan + gy % fan
        leading = (
            (first_block(lb) * n_gx + gy // fan).astype(jnp.float32) + 0.5
        ) * (N / (MX * n_gx)) - N / 2
        for j in range(n_gy):
            wait_bytes(y_in.at[slot, j], recv_b.at[slot, j])

        held, target = y_in.at[slot], y_a
        for level in range(y_bits):
            halves = n_gy >> level + 1
            width = N / (MY * 2**level)
            start = sum(n_gy >> k for k in range(level))
            last = level == y_bits - 1

            def unit(t, carry, held=held, target=target, halves=halves, width=width,
                     start=start, level=level, last=last):
                if last:
                    peer = (gy + n_gy // 2 + t) % n_gy
                    u = reverse(peer)
                else:
                    u = t
                box = u % halves
                path = u // halves
                sign = (1 - 2 * (path % 2)).astype(jnp.float32)
                centre = (
                    (lane_b * 2**level + path // 2).astype(jnp.float32) + 0.5
                ) * width - N / 2
                bending = bend_factor(centre, leading, sign * (width / 4))
                at = path // 2 * (2 * halves) + 2 * box

                def load(c, r, s):
                    if level == 0:
                        return held[at + c, pl.ds(r * 64 + s, 8, stride=8), :]
                    return held[at + c, r * 64 + s * 8 : r * 64 + s * 8 + 8, :]

                def coef(c, s):
                    return cy[start + 2 * box + c, pl.ds(s, 8, stride=8), :]

                def store(r, b, value):
                    if last:
                        y_t[pl.ds(r * 64 + b, 8, stride=8), :] = value
                    else:
                        target[u, r * 64 + b * 8 : r * 64 + b * 8 + 8, :] = value

                scale = sign * (width / 4 * 2**level / n_gy)
                merge(load, coef, bending, scale, box.astype(jnp.float32), store)
                if last:
                    y_out[slot, peer] = y_t[...].T.reshape(rows, MY, LANES)

                    @pl.when(peer == gy)
                    def _():
                        third_copy(slot, peer, True).start()

                    @pl.when(peer != gy)
                    def _():
                        third_copy(slot, peer, False).start()

                return carry

            lax.fori_loop(0, n_gy, unit, 0)
            held, target = target, (y_b if target is y_a else y_a)
        return carry

    lax.fori_loop(0, n_slot, y_block, 0)

    for lb in range(n_lb):
        for step in range(1, n_gx):
            first_copy(lb, step).wait_send()
        for step in range(n_gx):
            peer = second_peer(lb, step)

            @pl.when(peer != gy)
            def _():
                second_copy(lb, peer, False).wait_send()

    for slot in range(n_slot):
        for step in range(1, n_gy):
            third_copy(slot, (gy + step) % n_gy, False).wait_send()
        for j in range(n_gy):
            wait_bytes(o_ref.at[slot * fan + j % fan, :, j // fan], recv_c.at[slot, j])


def by_blocks(weights, coef_first, coef_second):
    n_gx = lax.axis_size("gx")
    n_gy = lax.axis_size("gy")
    per_gx = MX // n_gx
    rows = LANES // MY
    n_lb = per_gx // rows
    n_slot = n_lb // (n_gy // n_gx)
    block = (LANES, LANES)
    vmem = functools.partial(pltpu.VMEM, dtype=jnp.float32)
    dma = pltpu.SemaphoreType.DMA
    table_first = coef_first[0]
    finished = pl.pallas_call(
        functools.partial(butterfly_kernel, n_gx, n_gy),
        out_shape=jax.ShapeDtypeStruct((n_lb, rows, n_gx, MY, LANES), jnp.float32),
        in_specs=[
            pl.BlockSpec(memory_space=pl.ANY),
            pl.BlockSpec(memory_space=pltpu.VMEM),
            pl.BlockSpec(memory_space=pltpu.VMEM),
        ],
        out_specs=pl.BlockSpec(memory_space=pl.ANY),
        scratch_shapes=[
            vmem((n_gx, n_lb) + block),
            vmem((n_gx,) + block),
            vmem((n_gx,) + block),
            vmem((n_lb, n_gx) + block),
            vmem((n_slot, n_gy) + block),
            vmem((n_gy,) + block),
            vmem((n_gy,) + block),
            vmem(block),
            vmem((n_slot, n_gy, rows, MY, LANES)),
            vmem((table_first.shape[0], 64, LANES)),
            vmem((coef_second.shape[0], 64, LANES)),
            dma((n_lb, n_gx)),
            dma((n_lb, n_gx)),
            dma((n_lb, n_gx)),
            dma((n_slot, n_gy)),
            dma((n_slot, n_gy)),
            dma((n_slot, n_gy)),
        ],
        compiler_params=pltpu.CompilerParams(
            collective_id=0, has_side_effects=True, vmem_limit_bytes=56 * 2**20
        ),
        name="butterfly",
    )(weights.reshape(n_gx * n_lb, LANES, LANES), table_first, coef_second)
    return finished.reshape(1, per_gx * n_gx, MY, LANES)


def solution(mesh):
    in_specs = (P("gx", "gy", None, None, None), P("gy", None, None), P())
    out_specs = P("gy", "gx", None, None)
    fits = blocks_fit(mesh.shape["gx"], mesh.shape["gy"])
    return jax.shard_map(
        by_blocks if fits else on_device,
        mesh=mesh,
        in_specs=in_specs,
        out_specs=out_specs,
        check_vma=False,
    )
```

```python
import functools
import math

import jax
import jax.numpy as jnp
import numpy as np
from jax import lax
from jax.experimental import pallas as pl
from jax.experimental.pallas import tpu as pltpu
from jax.sharding import PartitionSpec as P

N = 4096
MX = 64
MY = 32


TWO_PI = 2.0 * math.pi


def from_partner(value, axis, apart):
    mask = 2**apart
    pairs = [(source, source ^ mask) for source in range(lax.axis_size(axis))]
    return lax.ppermute(value, axis, pairs)


def cheb_nodes():
    return np.cos(np.pi * (2.0 * np.arange(8) + 1.0) / 16.0)


def lagrange_child(child_half):
    nodes = cheb_nodes()
    targets = (2.0 * child_half - 1.0) / 2.0 + nodes / 2.0
    result = np.ones((8, 8))
    for target in range(8):
        for factor in range(8):
            if factor != target:
                result[target, :] = (
                    result[target, :] * (targets - nodes[factor]) / (nodes[target] - nodes[factor])
                )
    return result


def kron_stack(along_second):
    matrices = []
    for child_half in range(2):
        lagrange = lagrange_child(child_half)
        if along_second:
            middle = np.kron(np.eye(8), lagrange)
        else:
            middle = np.kron(lagrange, np.eye(8))
        matrices.append(np.kron(np.eye(2), middle).T)
    return jnp.asarray(np.stack(matrices), dtype=jnp.float32)


def node_pattern(along_second):
    nodes = cheb_nodes()
    if along_second:
        layout = np.tile(nodes, 8)
    else:
        layout = np.repeat(nodes, 8)
    return jnp.asarray(layout, dtype=jnp.float32)


def rotate_apply(values, phases, kernel):
    angles = phases * TWO_PI
    cosine = jnp.cos(angles)
    sines = jnp.sin(angles)
    real_part = values[..., :64]
    imag_part = values[..., 64:]
    rotated = jnp.concatenate(
        [cosine * real_part - sines * imag_part, sines * real_part + cosine * imag_part], axis=-1
    )
    mapped = jnp.dot(
        rotated.reshape(-1, 128),
        kernel,
        precision=lax.Precision.HIGHEST,
        preferred_element_type=jnp.float32,
    )
    return mapped.reshape(values.shape)


def bend_factor(centre, across, offset):
    shifted = centre - offset
    return (
        offset
        * (centre + shifted)
        / (
            jnp.sqrt(centre * centre + across * across)
            + jnp.sqrt(shifted * shifted + across * across)
        )
    )


def path_bits(device_pos, level_num):
    result = jnp.int32(0)
    for shift in range(level_num):
        result = result + ((device_pos >> shift & 1) << level_num - 1 - shift)
    return result


def x_term(current, table_rows, level_num, path_value, box_pos, pick_half, n_gx):
    freq_boxes = current.shape[0]
    columns = current.shape[1]
    box_width = N / (MX * 2**level_num)
    kernels = kron_stack(False)
    pattern = node_pattern(False)
    centre = (
        (jnp.arange(freq_boxes) * 2**level_num + path_value).astype(jnp.float32) + 0.5
    ) * box_width - N / 2
    across = (jnp.arange(columns).astype(jnp.float32) + 0.5) * (N / MY) - N / 2
    offset = box_width / 4 * (1 - 2 * pick_half).astype(jnp.float32)
    bending = bend_factor(centre[:, None], across[None, :], offset)
    location = (box_pos.astype(jnp.float32) + 0.5 + 0.5 * pattern) * (2**level_num / n_gx)
    start_row = sum((n_gx >> shift for shift in range(level_num)))
    coef_row = lax.dynamic_index_in_dim(table_rows, start_row + box_pos, 0, keepdims=False)
    phases = location[None, None, :] * offset + coef_row[None, None, :] * bending[:, :, None]
    return rotate_apply(current, phases, kernels[box_pos % 2])


def y_term(current, table_rows, level_num, path_value, box_pos, pick_half, n_gy, m_start, n_gx):
    row_count = current.shape[0]
    freq_boxes = current.shape[1]
    box_width = N / (MY * 2**level_num)
    kernels = kron_stack(True)
    pattern = node_pattern(True)
    leading = ((m_start + jnp.arange(row_count)).astype(jnp.float32) + 0.5) * (
        N / (MX * n_gx)
    ) - N / 2
    centre = (
        (jnp.arange(freq_boxes) * 2**level_num + path_value).astype(jnp.float32) + 0.5
    ) * box_width - N / 2
    offset = box_width / 4 * (1 - 2 * pick_half).astype(jnp.float32)
    bending = bend_factor(centre[None, :], leading[:, None], offset)
    location = (box_pos.astype(jnp.float32) + 0.5 + 0.5 * pattern) * (2**level_num / n_gy)
    start_row = sum((n_gy >> shift for shift in range(level_num)))
    coef_row = lax.dynamic_index_in_dim(table_rows, start_row + box_pos, 0, keepdims=False)
    phases = location[None, None, :] * offset + coef_row[None, None, :] * bending[:, :, None]
    return rotate_apply(current, phases, kernels[box_pos % 2])


def on_device(weights, coef_first, coef_second):
    n_gx = lax.axis_size("gx")
    n_gy = lax.axis_size("gy")
    x_bits = n_gx.bit_length() - 1
    y_bits = n_gy.bit_length() - 1
    gx_index = lax.axis_index("gx")
    gy_index = lax.axis_index("gy")
    table_first = coef_first[0]
    current = weights[0, 0]
    per_block = MX // n_gx
    for level_num in range(x_bits):
        box_pos = gx_index >> level_num
        own_half = box_pos % 2
        path_value = path_bits(gx_index, level_num)
        partner = from_partner(current, "gx", level_num)
        current = x_term(
            current, table_first, level_num, path_value, box_pos, own_half, n_gx
        ) + x_term(partner, table_first, level_num, path_value, box_pos ^ 1, own_half, n_gx)
    blocks = current.reshape(n_gx, per_block, MY, 128)
    gathered = lax.all_to_all(blocks, "gx", split_axis=0, concat_axis=0, tiled=True)
    gathered = gathered.reshape((2,) * x_bits + (per_block, MY, 128))
    gathered = jnp.transpose(
        gathered, tuple(reversed(range(x_bits))) + tuple(range(x_bits, x_bits + 3))
    )
    gathered = gathered.reshape(n_gx, per_block, MY, 128)
    current = jnp.transpose(gathered, (1, 0, 2, 3)).reshape(MX, MY, 128)
    m_start = gx_index * MX
    for level_num in range(y_bits):
        box_pos = gy_index >> level_num
        own_half = box_pos % 2
        path_value = path_bits(gy_index, level_num)
        partner = from_partner(current, "gy", level_num)
        current = y_term(
            current, coef_second, level_num, path_value, box_pos, own_half, n_gy, m_start, n_gx
        ) + y_term(
            partner, coef_second, level_num, path_value, box_pos ^ 1, own_half, n_gy, m_start, n_gx
        )
    return current[None]


LANES = 128
AHEAD = 1
HOLD = 0
MESH = pl.DeviceIdType.MESH


def blocks_fit(n_gx, n_gy):
    per_gx = MX // n_gx
    if MX % n_gx or (per_gx * MY) % LANES or LANES % MY or n_gy % n_gx:
        return False
    return (per_gx * MY // LANES) % (n_gy // n_gx) == 0


def chebyshev_fit(func, degree):
    grid = 0.25 * (1 + np.cos(np.pi * (np.arange(400) + 0.5) / 400)) * 0.5
    series = np.polynomial.chebyshev.Chebyshev.fit(grid, func(grid), degree, domain=[0.0, 0.25])
    return [float(c) for c in series.convert(kind=np.polynomial.Polynomial).coef]


def horner(coefs, arg):
    result = coefs[-1]
    for coef in coefs[-2::-1]:
        result = result * arg + coef
    return result


COS_FIT = chebyshev_fit(lambda t: np.cos(np.pi * np.sqrt(t)), 5)
SIN_FIT = chebyshev_fit(lambda t: 2.0 * np.sinc(np.sqrt(t)) * np.pi, 5)
ROUNDER = 1.5 * 2.0**23


def cos_sin_turns(turns):
    part = turns - ((turns + ROUNDER) - ROUNDER)
    square = part * part
    cos_half = horner(COS_FIT, square)
    twice_sin_half = horner(SIN_FIT, square) * part
    return 1.0 - 0.5 * (twice_sin_half * twice_sin_half), twice_sin_half * cos_half


def merge(load, coef, bending, scale, box, store):
    nodes = cheb_nodes()
    lagrange = lagrange_child(0)
    plus = [[None] * 4, [None] * 4]
    minus = [[None] * 4, [None] * 4]
    bases = [scale * (2 * box + c + 0.5) for c in range(2)]
    for s in range(8):
        rotated = []
        for c in range(2):
            at = s if c == 0 else 7 - s
            turns = coef(c, at) * bending + (bases[c] + scale * float(0.5 * nodes[at]))
            cosine, sine = cos_sin_turns(turns)
            real, imag = load(c, 0, at), load(c, 1, at)
            rotated.append((cosine * real - sine * imag, sine * real + cosine * imag))
        for r in range(2):
            total = rotated[0][r] + rotated[1][r]
            apart = rotated[0][r] - rotated[1][r]
            for a in range(4):
                even = total * float(0.5 * (lagrange[a, s] + lagrange[7 - a, s]))
                odd = apart * float(0.5 * (lagrange[a, s] - lagrange[7 - a, s]))
                plus[r][a] = even if s == 0 else plus[r][a] + even
                minus[r][a] = odd if s == 0 else minus[r][a] + odd
    for r in range(2):
        for a in range(4):
            store(r, a, plus[r][a] + minus[r][a])
            store(r, 7 - a, plus[r][a] - minus[r][a])


def wait_bytes(ref, sem):
    pltpu.make_async_copy(ref, ref, sem).wait()


def butterfly_kernel(
    n_gx, n_gy, w_ref, cf_ref, cs_ref, o_ref,
    x_in, x_a, x_b, x_out, y_in, y_a, y_b, y_t, y_out, cx, cy,
    send_a, recv_a, send_b, recv_b, send_c, recv_c,
):
    gx = lax.axis_index("gx")
    gy = lax.axis_index("gy")
    x_bits = n_gx.bit_length() - 1
    y_bits = n_gy.bit_length() - 1
    per_gx = MX // n_gx
    rows = LANES // MY
    n_lb = per_gx // rows
    fan = n_gy // n_gx
    n_slot = n_lb // fan

    barrier = pltpu.get_barrier_semaphore()
    for step in range(1, n_gx):
        pl.semaphore_signal(
            barrier, inc=1, device_id=((gx + step) % n_gx, gy), device_id_type=MESH
        )
    for step in range(1, n_gy):
        pl.semaphore_signal(
            barrier, inc=1, device_id=(gx, (gy + step) % n_gy), device_id_type=MESH
        )
    pl.semaphore_wait(barrier, n_gx + n_gy - 2)

    def first_copy(lb, step):
        peer = (gx + step) % n_gx
        return pltpu.make_async_remote_copy(
            src_ref=w_ref.at[peer * n_lb + lb],
            dst_ref=x_in.at[gx, lb],
            send_sem=send_a.at[lb, step],
            recv_sem=recv_a.at[lb, gx],
            device_id=(peer, gy),
            device_id_type=MESH,
        )

    def first_start(lb):
        for step in range(1, n_gx):
            first_copy(lb, step).start()
        pltpu.make_async_copy(
            w_ref.at[gx * n_lb + lb], x_in.at[gx, lb], recv_a.at[lb, gx]
        ).start()

    for lb in range(min(AHEAD, n_lb)):
        first_start(lb)

    for source, spread in ((cf_ref, cx), (cs_ref, cy)):
        for row in range(source.shape[0]):
            line = jnp.broadcast_to(source[row].reshape(1, 64), (LANES, 64))
            spread[row] = line.T

    lane = lax.broadcasted_iota(jnp.int32, (8, LANES), 1)
    lane_m = lane // MY
    lane_b = lane % MY
    second = (lane_b.astype(jnp.float32) + 0.5) * (N / MY) - N / 2

    def first_block(lb):
        return gx * per_gx + lb * rows + lane_m

    def second_peer(lb, step):
        return (gy // fan + step) % n_gx * fan + lb % fan

    def second_copy(lb, peer, gets_local):
        z = peer // fan
        slot = lb // fan
        if gets_local:
            return pltpu.make_async_copy(
                x_out.at[lb, z], y_in.at[slot, gy], recv_b.at[slot, gy]
            )
        return pltpu.make_async_remote_copy(
            src_ref=x_out.at[lb, z],
            dst_ref=y_in.at[slot, gy],
            send_sem=send_b.at[lb, z],
            recv_sem=recv_b.at[slot, gy],
            device_id=(gx, peer),
            device_id_type=MESH,
        )

    def x_block(lb, carry):
        for i in range(n_gx):
            wait_bytes(x_in.at[i, lb], recv_a.at[lb, i])

        @pl.when(lb + AHEAD < n_lb)
        def _():
            first_start(lb + AHEAD)

        def turn(i, carry):
            x_a[i] = x_in[i, lb].T
            return carry

        lax.fori_loop(0, n_gx, turn, 0)
        held, other = x_a, x_b
        for level in range(x_bits):
            halves = n_gx >> level + 1
            width = N / (MX * 2**level)
            start = sum(n_gx >> k for k in range(level))
            last = level == x_bits - 1
            target = x_out.at[lb] if last else other

            def unit(u, carry, held=held, target=target, halves=halves, width=width,
                     start=start, level=level):
                box = u % halves
                path = u // halves
                sign = (1 - 2 * (path % 2)).astype(jnp.float32)
                centre = (
                    (first_block(lb) * 2**level + path // 2).astype(jnp.float32) + 0.5
                ) * width - N / 2
                bending = bend_factor(centre, second, sign * (width / 4))
                at = path // 2 * (2 * halves) + 2 * box

                def load(c, r, s):
                    return held[at + c, r * 64 + s * 8 : r * 64 + s * 8 + 8, :]

                def coef(c, s):
                    return cx[start + 2 * box + c, s * 8 : s * 8 + 8, :]

                def store(r, a, value):
                    target[u, r * 64 + a * 8 : r * 64 + a * 8 + 8, :] = value

                scale = sign * (width / 4 * 2**level / n_gx)
                merge(load, coef, bending, scale, box.astype(jnp.float32), store)
                return carry

            lax.fori_loop(0, n_gx, unit, 0)
            held, other = target, held

        def send(step, carry):
            peer = second_peer(lb, step + n_gx // 2)

            @pl.when(peer == gy)
            def _():
                second_copy(lb, peer, True).start()

            @pl.when(peer != gy)
            def _():
                second_copy(lb, peer, False).start()

            return carry

        lax.fori_loop(0, n_gx, send, 0)
        return carry

    lax.fori_loop(0, n_lb, x_block, 0)

    def reverse(value):
        result = 0
        for shift in range(y_bits):
            result = result * 2 + value // 2**shift % 2
        return result

    def third_copy(slot, peer, gets_local):
        here = slot * fan + gy % fan
        place = o_ref.at[here, :, gy // fan]
        if gets_local:
            return pltpu.make_async_copy(y_out.at[slot, peer], place, recv_c.at[slot, gy])
        return pltpu.make_async_remote_copy(
            src_ref=y_out.at[slot, peer],
            dst_ref=place,
            send_sem=send_c.at[slot, peer],
            recv_sem=recv_c.at[slot, gy],
            device_id=(gx, peer),
            device_id_type=MESH,
        )

    def third_start(slot, peer):
        @pl.when(peer == gy)
        def _():
            third_copy(slot, peer, True).start()

        @pl.when(peer != gy)
        def _():
            third_copy(slot, peer, False).start()

    def y_block(slot, carry):
        lb = slot * fan + gy % fan
        leading = (
            (first_block(lb) * n_gx + gy // fan).astype(jnp.float32) + 0.5
        ) * (N / (MX * n_gx)) - N / 2
        for j in range(n_gy):
            wait_bytes(y_in.at[slot, j], recv_b.at[slot, j])

        def held_back(t, carry):
            third_start(slot - 1, (gy + n_gy // 2 + t) % n_gy)
            return carry

        @pl.when((slot >= 1) & (slot <= HOLD))
        def _():
            lax.fori_loop(0, n_gy, held_back, 0)

        held, target = y_in.at[slot], y_a
        for level in range(y_bits):
            halves = n_gy >> level + 1
            width = N / (MY * 2**level)
            start = sum(n_gy >> k for k in range(level))
            last = level == y_bits - 1

            def unit(t, carry, held=held, target=target, halves=halves, width=width,
                     start=start, level=level, last=last):
                if last:
                    peer = (gy + n_gy // 2 + t) % n_gy
                    u = reverse(peer)
                else:
                    u = t
                box = u % halves
                path = u // halves
                sign = (1 - 2 * (path % 2)).astype(jnp.float32)
                centre = (
                    (lane_b * 2**level + path // 2).astype(jnp.float32) + 0.5
                ) * width - N / 2
                bending = bend_factor(centre, leading, sign * (width / 4))
                at = path // 2 * (2 * halves) + 2 * box

                def load(c, r, s):
                    if level == 0:
                        return held[at + c, pl.ds(r * 64 + s, 8, stride=8), :]
                    return held[at + c, r * 64 + s * 8 : r * 64 + s * 8 + 8, :]

                def coef(c, s):
                    return cy[start + 2 * box + c, pl.ds(s, 8, stride=8), :]

                def store(r, b, value):
                    if last:
                        y_t[pl.ds(r * 64 + b, 8, stride=8), :] = value
                    else:
                        target[u, r * 64 + b * 8 : r * 64 + b * 8 + 8, :] = value

                scale = sign * (width / 4 * 2**level / n_gy)
                merge(load, coef, bending, scale, box.astype(jnp.float32), store)
                if last:
                    y_out[slot, peer] = y_t[...].T.reshape(rows, MY, LANES)

                    @pl.when(slot >= HOLD)
                    def _():
                        third_start(slot, peer)

                return carry

            lax.fori_loop(0, n_gy, unit, 0)
            held, target = target, (y_b if target is y_a else y_a)
        return carry

    lax.fori_loop(0, n_slot, y_block, 0)

    for lb in range(n_lb):
        for step in range(1, n_gx):
            first_copy(lb, step).wait_send()
        for step in range(n_gx):
            peer = second_peer(lb, step)

            @pl.when(peer != gy)
            def _():
                second_copy(lb, peer, False).wait_send()

    for slot in range(n_slot):
        for step in range(1, n_gy):
            third_copy(slot, (gy + step) % n_gy, False).wait_send()
        for j in range(n_gy):
            wait_bytes(o_ref.at[slot * fan + j % fan, :, j // fan], recv_c.at[slot, j])


def by_blocks(weights, coef_first, coef_second):
    n_gx = lax.axis_size("gx")
    n_gy = lax.axis_size("gy")
    per_gx = MX // n_gx
    rows = LANES // MY
    n_lb = per_gx // rows
    n_slot = n_lb // (n_gy // n_gx)
    block = (LANES, LANES)
    vmem = functools.partial(pltpu.VMEM, dtype=jnp.float32)
    dma = pltpu.SemaphoreType.DMA
    table_first = jnp.transpose(coef_first, (1, 0, 2))
    finished = pl.pallas_call(
        functools.partial(butterfly_kernel, n_gx, n_gy),
        out_shape=jax.ShapeDtypeStruct((n_lb, rows, n_gx, MY, LANES), jnp.float32),
        in_specs=[
            pl.BlockSpec(memory_space=pltpu.HBM),
            pl.BlockSpec(memory_space=pltpu.VMEM),
            pl.BlockSpec(memory_space=pltpu.VMEM),
        ],
        out_specs=pl.BlockSpec(memory_space=pl.ANY),
        scratch_shapes=[
            vmem((n_gx, n_lb) + block),
            vmem((n_gx,) + block),
            vmem((n_gx,) + block),
            vmem((n_lb, n_gx) + block),
            vmem((n_slot, n_gy) + block),
            vmem((n_gy,) + block),
            vmem((n_gy,) + block),
            vmem(block),
            vmem((n_slot, n_gy, rows, MY, LANES)),
            vmem((table_first.shape[0], 64, LANES)),
            vmem((coef_second.shape[0], 64, LANES)),
            dma((n_lb, n_gx)),
            dma((n_lb, n_gx)),
            dma((n_lb, n_gx)),
            dma((n_slot, n_gy)),
            dma((n_slot, n_gy)),
            dma((n_slot, n_gy)),
        ],
        compiler_params=pltpu.CompilerParams(
            collective_id=0, has_side_effects=True, vmem_limit_bytes=52 * 2**20
        ),
        name="butterfly",
    )(weights.reshape(n_gx * n_lb, LANES, LANES), table_first, coef_second)
    return finished.reshape(1, per_gx * n_gx, MY, LANES)


def solution(mesh):
    in_specs = (P("gx", "gy", None, None, None), P("gy", None, None), P())
    out_specs = P("gy", "gx", None, None)
    fits = blocks_fit(mesh.shape["gx"], mesh.shape["gy"])
    return jax.shard_map(
        by_blocks if fits else on_device,
        mesh=mesh,
        in_specs=in_specs,
        out_specs=out_specs,
        check_vma=False,
    )
```

```python
import functools
import math

import jax
import jax.numpy as jnp
import numpy as np
from jax import lax
from jax.experimental import pallas as pl
from jax.experimental.pallas import tpu as pltpu
from jax.sharding import PartitionSpec as P

N = 4096
MX = 64
MY = 32


TWO_PI = 2.0 * math.pi


def from_partner(value, axis, apart):
    mask = 2**apart
    pairs = [(source, source ^ mask) for source in range(lax.axis_size(axis))]
    return lax.ppermute(value, axis, pairs)


def cheb_nodes():
    return np.cos(np.pi * (2.0 * np.arange(8) + 1.0) / 16.0)


def lagrange_child(child_half):
    nodes = cheb_nodes()
    targets = (2.0 * child_half - 1.0) / 2.0 + nodes / 2.0
    result = np.ones((8, 8))
    for target in range(8):
        for factor in range(8):
            if factor != target:
                result[target, :] = (
                    result[target, :] * (targets - nodes[factor]) / (nodes[target] - nodes[factor])
                )
    return result


def kron_stack(along_second):
    matrices = []
    for child_half in range(2):
        lagrange = lagrange_child(child_half)
        if along_second:
            middle = np.kron(np.eye(8), lagrange)
        else:
            middle = np.kron(lagrange, np.eye(8))
        matrices.append(np.kron(np.eye(2), middle).T)
    return jnp.asarray(np.stack(matrices), dtype=jnp.float32)


def node_pattern(along_second):
    nodes = cheb_nodes()
    if along_second:
        layout = np.tile(nodes, 8)
    else:
        layout = np.repeat(nodes, 8)
    return jnp.asarray(layout, dtype=jnp.float32)


def rotate_apply(values, phases, kernel):
    angles = phases * TWO_PI
    cosine = jnp.cos(angles)
    sines = jnp.sin(angles)
    real_part = values[..., :64]
    imag_part = values[..., 64:]
    rotated = jnp.concatenate(
        [cosine * real_part - sines * imag_part, sines * real_part + cosine * imag_part], axis=-1
    )
    mapped = jnp.dot(
        rotated.reshape(-1, 128),
        kernel,
        precision=lax.Precision.HIGHEST,
        preferred_element_type=jnp.float32,
    )
    return mapped.reshape(values.shape)


def bend_factor(centre, across, offset):
    shifted = centre - offset
    return (
        offset
        * (centre + shifted)
        / (
            jnp.sqrt(centre * centre + across * across)
            + jnp.sqrt(shifted * shifted + across * across)
        )
    )


def path_bits(device_pos, level_num):
    result = jnp.int32(0)
    for shift in range(level_num):
        result = result + ((device_pos >> shift & 1) << level_num - 1 - shift)
    return result


def x_term(current, table_rows, level_num, path_value, box_pos, pick_half, n_gx):
    freq_boxes = current.shape[0]
    columns = current.shape[1]
    box_width = N / (MX * 2**level_num)
    kernels = kron_stack(False)
    pattern = node_pattern(False)
    centre = (
        (jnp.arange(freq_boxes) * 2**level_num + path_value).astype(jnp.float32) + 0.5
    ) * box_width - N / 2
    across = (jnp.arange(columns).astype(jnp.float32) + 0.5) * (N / MY) - N / 2
    offset = box_width / 4 * (1 - 2 * pick_half).astype(jnp.float32)
    bending = bend_factor(centre[:, None], across[None, :], offset)
    location = (box_pos.astype(jnp.float32) + 0.5 + 0.5 * pattern) * (2**level_num / n_gx)
    start_row = sum((n_gx >> shift for shift in range(level_num)))
    coef_row = lax.dynamic_index_in_dim(table_rows, start_row + box_pos, 0, keepdims=False)
    phases = location[None, None, :] * offset + coef_row[None, None, :] * bending[:, :, None]
    return rotate_apply(current, phases, kernels[box_pos % 2])


def y_term(current, table_rows, level_num, path_value, box_pos, pick_half, n_gy, m_start, n_gx):
    row_count = current.shape[0]
    freq_boxes = current.shape[1]
    box_width = N / (MY * 2**level_num)
    kernels = kron_stack(True)
    pattern = node_pattern(True)
    leading = ((m_start + jnp.arange(row_count)).astype(jnp.float32) + 0.5) * (
        N / (MX * n_gx)
    ) - N / 2
    centre = (
        (jnp.arange(freq_boxes) * 2**level_num + path_value).astype(jnp.float32) + 0.5
    ) * box_width - N / 2
    offset = box_width / 4 * (1 - 2 * pick_half).astype(jnp.float32)
    bending = bend_factor(centre[None, :], leading[:, None], offset)
    location = (box_pos.astype(jnp.float32) + 0.5 + 0.5 * pattern) * (2**level_num / n_gy)
    start_row = sum((n_gy >> shift for shift in range(level_num)))
    coef_row = lax.dynamic_index_in_dim(table_rows, start_row + box_pos, 0, keepdims=False)
    phases = location[None, None, :] * offset + coef_row[None, None, :] * bending[:, :, None]
    return rotate_apply(current, phases, kernels[box_pos % 2])


def on_device(weights, coef_first, coef_second):
    n_gx = lax.axis_size("gx")
    n_gy = lax.axis_size("gy")
    x_bits = n_gx.bit_length() - 1
    y_bits = n_gy.bit_length() - 1
    gx_index = lax.axis_index("gx")
    gy_index = lax.axis_index("gy")
    table_first = coef_first[0]
    current = weights[0, 0]
    per_block = MX // n_gx
    for level_num in range(x_bits):
        box_pos = gx_index >> level_num
        own_half = box_pos % 2
        path_value = path_bits(gx_index, level_num)
        partner = from_partner(current, "gx", level_num)
        current = x_term(
            current, table_first, level_num, path_value, box_pos, own_half, n_gx
        ) + x_term(partner, table_first, level_num, path_value, box_pos ^ 1, own_half, n_gx)
    blocks = current.reshape(n_gx, per_block, MY, 128)
    gathered = lax.all_to_all(blocks, "gx", split_axis=0, concat_axis=0, tiled=True)
    gathered = gathered.reshape((2,) * x_bits + (per_block, MY, 128))
    gathered = jnp.transpose(
        gathered, tuple(reversed(range(x_bits))) + tuple(range(x_bits, x_bits + 3))
    )
    gathered = gathered.reshape(n_gx, per_block, MY, 128)
    current = jnp.transpose(gathered, (1, 0, 2, 3)).reshape(MX, MY, 128)
    m_start = gx_index * MX
    for level_num in range(y_bits):
        box_pos = gy_index >> level_num
        own_half = box_pos % 2
        path_value = path_bits(gy_index, level_num)
        partner = from_partner(current, "gy", level_num)
        current = y_term(
            current, coef_second, level_num, path_value, box_pos, own_half, n_gy, m_start, n_gx
        ) + y_term(
            partner, coef_second, level_num, path_value, box_pos ^ 1, own_half, n_gy, m_start, n_gx
        )
    return current[None]


LANES = 128
AHEAD = 1
HOLD = 0
MESH = pl.DeviceIdType.MESH


def blocks_fit(n_gx, n_gy):
    per_gx = MX // n_gx
    if MX % n_gx or (per_gx * MY) % LANES or LANES % MY or n_gy % n_gx:
        return False
    return (per_gx * MY // LANES) % (n_gy // n_gx) == 0


def chebyshev_fit(func, degree):
    grid = 0.25 * (1 + np.cos(np.pi * (np.arange(400) + 0.5) / 400)) * 0.5
    series = np.polynomial.chebyshev.Chebyshev.fit(grid, func(grid), degree, domain=[0.0, 0.25])
    return [float(c) for c in series.convert(kind=np.polynomial.Polynomial).coef]


def horner(coefs, arg):
    result = coefs[-1]
    for coef in coefs[-2::-1]:
        result = result * arg + coef
    return result


COS_FIT = chebyshev_fit(lambda t: np.cos(np.pi * np.sqrt(t)), 5)
SIN_FIT = chebyshev_fit(lambda t: 2.0 * np.sinc(np.sqrt(t)) * np.pi, 5)
ROUNDER = 1.5 * 2.0**23


def cos_sin_turns(turns):
    part = turns - ((turns + ROUNDER) - ROUNDER)
    square = part * part
    cos_half = horner(COS_FIT, square)
    twice_sin_half = horner(SIN_FIT, square) * part
    return 1.0 - 0.5 * (twice_sin_half * twice_sin_half), twice_sin_half * cos_half


def merge(load, coef, bending, scale, box, store):
    nodes = cheb_nodes()
    lagrange = lagrange_child(0)
    plus = [[None] * 4, [None] * 4]
    minus = [[None] * 4, [None] * 4]
    bases = [scale * (2 * box + c + 0.5) for c in range(2)]
    for s in range(8):
        rotated = []
        for c in range(2):
            at = s if c == 0 else 7 - s
            turns = coef(c, at) * bending + (bases[c] + scale * float(0.5 * nodes[at]))
            cosine, sine = cos_sin_turns(turns)
            real, imag = load(c, 0, at), load(c, 1, at)
            rotated.append((cosine * real - sine * imag, sine * real + cosine * imag))
        for r in range(2):
            total = rotated[0][r] + rotated[1][r]
            apart = rotated[0][r] - rotated[1][r]
            for a in range(4):
                even = total * float(0.5 * (lagrange[a, s] + lagrange[7 - a, s]))
                odd = apart * float(0.5 * (lagrange[a, s] - lagrange[7 - a, s]))
                plus[r][a] = even if s == 0 else plus[r][a] + even
                minus[r][a] = odd if s == 0 else minus[r][a] + odd
    for r in range(2):
        for a in range(4):
            store(r, a, plus[r][a] + minus[r][a])
            store(r, 7 - a, plus[r][a] - minus[r][a])


def wait_bytes(ref, sem):
    pltpu.make_async_copy(ref, ref, sem).wait()


def butterfly_kernel(
    n_gx, n_gy, w_ref, cf_ref, cs_ref, o_ref,
    x_in, x_a, x_b, x_out, y_in, y_a, y_b, y_t, y_out, cx, cy,
    send_a, recv_a, send_b, recv_b, send_c, recv_c,
):
    gx = lax.axis_index("gx")
    gy = lax.axis_index("gy")
    x_bits = n_gx.bit_length() - 1
    y_bits = n_gy.bit_length() - 1
    per_gx = MX // n_gx
    rows = LANES // MY
    n_lb = per_gx // rows
    fan = n_gy // n_gx
    n_slot = n_lb // fan

    barrier = pltpu.get_barrier_semaphore()
    for step in range(1, n_gx):
        pl.semaphore_signal(
            barrier, inc=1, device_id=((gx + step) % n_gx, gy), device_id_type=MESH
        )
    for step in range(1, n_gy):
        pl.semaphore_signal(
            barrier, inc=1, device_id=(gx, (gy + step) % n_gy), device_id_type=MESH
        )
    pl.semaphore_wait(barrier, n_gx + n_gy - 2)

    def first_copy(lb, step):
        peer = (gx + step) % n_gx
        return pltpu.make_async_remote_copy(
            src_ref=w_ref.at[peer * n_lb + lb],
            dst_ref=x_in.at[gx, lb],
            send_sem=send_a.at[lb, step],
            recv_sem=recv_a.at[lb, gx],
            device_id=(peer, gy),
            device_id_type=MESH,
        )

    def first_start(lb):
        for step in range(1, n_gx):
            first_copy(lb, step).start()
        pltpu.make_async_copy(
            w_ref.at[gx * n_lb + lb], x_in.at[gx, lb], recv_a.at[lb, gx]
        ).start()

    for lb in range(min(AHEAD, n_lb)):
        first_start(lb)

    for source, spread in ((cf_ref, cx), (cs_ref, cy)):
        for row in range(source.shape[0]):
            line = jnp.broadcast_to(source[row].reshape(1, 64), (LANES, 64))
            spread[row] = line.T

    lane = lax.broadcasted_iota(jnp.int32, (8, LANES), 1)
    lane_m = lane // MY
    lane_b = lane % MY
    second = (lane_b.astype(jnp.float32) + 0.5) * (N / MY) - N / 2

    def first_block(lb):
        return gx * per_gx + lb * rows + lane_m

    def second_peer(lb, step):
        return (gy // fan + step) % n_gx * fan + lb % fan

    def second_copy(lb, peer, gets_local):
        z = peer // fan
        slot = lb // fan
        if gets_local:
            return pltpu.make_async_copy(
                x_out.at[lb, z], y_in.at[slot, gy], recv_b.at[slot, gy]
            )
        return pltpu.make_async_remote_copy(
            src_ref=x_out.at[lb, z],
            dst_ref=y_in.at[slot, gy],
            send_sem=send_b.at[lb, z],
            recv_sem=recv_b.at[slot, gy],
            device_id=(gx, peer),
            device_id_type=MESH,
        )

    def second_start(lb, peer):
        @pl.when(peer == gy)
        def _():
            second_copy(lb, peer, True).start()

        @pl.when(peer != gy)
        def _():
            second_copy(lb, peer, False).start()

    def x_block(lb, carry):
        for i in range(n_gx):
            wait_bytes(x_in.at[i, lb], recv_a.at[lb, i])

        @pl.when(lb + AHEAD < n_lb)
        def _():
            first_start(lb + AHEAD)

        def turn(i, carry):
            x_a[i] = x_in[i, lb].T
            return carry

        lax.fori_loop(0, n_gx, turn, 0)
        held, other = x_a, x_b
        for level in range(x_bits):
            halves = n_gx >> level + 1
            width = N / (MX * 2**level)
            start = sum(n_gx >> k for k in range(level))
            last = level == x_bits - 1
            target = x_out.at[lb] if last else other

            def unit(t, carry, held=held, target=target, halves=halves, width=width,
                     start=start, level=level, last=last):
                u = (gy // fan + n_gx // 2 + t) % n_gx if last else t
                box = u % halves
                path = u // halves
                sign = (1 - 2 * (path % 2)).astype(jnp.float32)
                centre = (
                    (first_block(lb) * 2**level + path // 2).astype(jnp.float32) + 0.5
                ) * width - N / 2
                bending = bend_factor(centre, second, sign * (width / 4))
                at = path // 2 * (2 * halves) + 2 * box

                def load(c, r, s):
                    return held[at + c, r * 64 + s * 8 : r * 64 + s * 8 + 8, :]

                def coef(c, s):
                    return cx[start + 2 * box + c, s * 8 : s * 8 + 8, :]

                def store(r, a, value):
                    target[u, r * 64 + a * 8 : r * 64 + a * 8 + 8, :] = value

                scale = sign * (width / 4 * 2**level / n_gx)
                merge(load, coef, bending, scale, box.astype(jnp.float32), store)
                if last:
                    second_start(lb, u * fan + lb % fan)
                return carry

            lax.fori_loop(0, n_gx, unit, 0)
            held, other = target, held

        return carry

    lax.fori_loop(0, n_lb, x_block, 0)

    def reverse(value):
        result = 0
        for shift in range(y_bits):
            result = result * 2 + value // 2**shift % 2
        return result

    def third_copy(slot, peer, gets_local):
        here = slot * fan + gy % fan
        place = o_ref.at[here, :, gy // fan]
        if gets_local:
            return pltpu.make_async_copy(y_out.at[slot, peer], place, recv_c.at[slot, gy])
        return pltpu.make_async_remote_copy(
            src_ref=y_out.at[slot, peer],
            dst_ref=place,
            send_sem=send_c.at[slot, peer],
            recv_sem=recv_c.at[slot, gy],
            device_id=(gx, peer),
            device_id_type=MESH,
        )

    def third_start(slot, peer):
        @pl.when(peer == gy)
        def _():
            third_copy(slot, peer, True).start()

        @pl.when(peer != gy)
        def _():
            third_copy(slot, peer, False).start()

    def y_block(slot, carry):
        lb = slot * fan + gy % fan
        leading = (
            (first_block(lb) * n_gx + gy // fan).astype(jnp.float32) + 0.5
        ) * (N / (MX * n_gx)) - N / 2
        for j in range(n_gy):
            wait_bytes(y_in.at[slot, j], recv_b.at[slot, j])

        def held_back(t, carry):
            third_start(slot - 1, (gy + n_gy // 2 + t) % n_gy)
            return carry

        @pl.when((slot >= 1) & (slot <= HOLD))
        def _():
            lax.fori_loop(0, n_gy, held_back, 0)

        held, target = y_in.at[slot], y_a
        for level in range(y_bits):
            halves = n_gy >> level + 1
            width = N / (MY * 2**level)
            start = sum(n_gy >> k for k in range(level))
            last = level == y_bits - 1

            def unit(t, carry, held=held, target=target, halves=halves, width=width,
                     start=start, level=level, last=last):
                if last:
                    peer = (gy + n_gy // 2 + t) % n_gy
                    u = reverse(peer)
                else:
                    u = t
                box = u % halves
                path = u // halves
                sign = (1 - 2 * (path % 2)).astype(jnp.float32)
                centre = (
                    (lane_b * 2**level + path // 2).astype(jnp.float32) + 0.5
                ) * width - N / 2
                bending = bend_factor(centre, leading, sign * (width / 4))
                at = path // 2 * (2 * halves) + 2 * box

                def load(c, r, s):
                    if level == 0:
                        return held[at + c, pl.ds(r * 64 + s, 8, stride=8), :]
                    return held[at + c, r * 64 + s * 8 : r * 64 + s * 8 + 8, :]

                def coef(c, s):
                    return cy[start + 2 * box + c, pl.ds(s, 8, stride=8), :]

                def store(r, b, value):
                    if last:
                        y_t[pl.ds(r * 64 + b, 8, stride=8), :] = value
                    else:
                        target[u, r * 64 + b * 8 : r * 64 + b * 8 + 8, :] = value

                scale = sign * (width / 4 * 2**level / n_gy)
                merge(load, coef, bending, scale, box.astype(jnp.float32), store)
                if last:
                    y_out[slot, peer] = y_t[...].T.reshape(rows, MY, LANES)

                    @pl.when(slot >= HOLD)
                    def _():
                        third_start(slot, peer)

                return carry

            lax.fori_loop(0, n_gy, unit, 0)
            held, target = target, (y_b if target is y_a else y_a)
        return carry

    lax.fori_loop(0, n_slot, y_block, 0)

    for lb in range(n_lb):
        for step in range(1, n_gx):
            first_copy(lb, step).wait_send()
        for step in range(n_gx):
            peer = second_peer(lb, step)

            @pl.when(peer != gy)
            def _():
                second_copy(lb, peer, False).wait_send()

    for slot in range(n_slot):
        for step in range(1, n_gy):
            third_copy(slot, (gy + step) % n_gy, False).wait_send()
        for j in range(n_gy):
            wait_bytes(o_ref.at[slot * fan + j % fan, :, j // fan], recv_c.at[slot, j])


def by_blocks(weights, coef_first, coef_second):
    n_gx = lax.axis_size("gx")
    n_gy = lax.axis_size("gy")
    per_gx = MX // n_gx
    rows = LANES // MY
    n_lb = per_gx // rows
    n_slot = n_lb // (n_gy // n_gx)
    block = (LANES, LANES)
    vmem = functools.partial(pltpu.VMEM, dtype=jnp.float32)
    dma = pltpu.SemaphoreType.DMA
    table_first = jnp.transpose(coef_first, (1, 0, 2))
    finished = pl.pallas_call(
        functools.partial(butterfly_kernel, n_gx, n_gy),
        out_shape=jax.ShapeDtypeStruct((n_lb, rows, n_gx, MY, LANES), jnp.float32),
        in_specs=[
            pl.BlockSpec(memory_space=pltpu.HBM),
            pl.BlockSpec(memory_space=pltpu.VMEM),
            pl.BlockSpec(memory_space=pltpu.VMEM),
        ],
        out_specs=pl.BlockSpec(memory_space=pl.ANY),
        scratch_shapes=[
            vmem((n_gx, n_lb) + block),
            vmem((n_gx,) + block),
            vmem((n_gx,) + block),
            vmem((n_lb, n_gx) + block),
            vmem((n_slot, n_gy) + block),
            vmem((n_gy,) + block),
            vmem((n_gy,) + block),
            vmem(block),
            vmem((n_slot, n_gy, rows, MY, LANES)),
            vmem((table_first.shape[0], 64, LANES)),
            vmem((coef_second.shape[0], 64, LANES)),
            dma((n_lb, n_gx)),
            dma((n_lb, n_gx)),
            dma((n_lb, n_gx)),
            dma((n_slot, n_gy)),
            dma((n_slot, n_gy)),
            dma((n_slot, n_gy)),
        ],
        compiler_params=pltpu.CompilerParams(
            collective_id=0, has_side_effects=True, vmem_limit_bytes=52 * 2**20
        ),
        name="butterfly",
    )(weights.reshape(n_gx * n_lb, LANES, LANES), table_first, coef_second)
    return finished.reshape(1, per_gx * n_gx, MY, LANES)


def solution(mesh):
    in_specs = (P("gx", "gy", None, None, None), P("gy", None, None), P())
    out_specs = P("gy", "gx", None, None)
    fits = blocks_fit(mesh.shape["gx"], mesh.shape["gy"])
    return jax.shard_map(
        by_blocks if fits else on_device,
        mesh=mesh,
        in_specs=in_specs,
        out_specs=out_specs,
        check_vma=False,
    )
```

```python
import functools
import math

import jax
import jax.numpy as jnp
import numpy as np
from jax import lax
from jax.experimental import pallas as pl
from jax.experimental.pallas import tpu as pltpu
from jax.sharding import PartitionSpec as P

N = 4096
MX = 64
MY = 32


TWO_PI = 2.0 * math.pi


def from_partner(value, axis, apart):
    mask = 2**apart
    pairs = [(source, source ^ mask) for source in range(lax.axis_size(axis))]
    return lax.ppermute(value, axis, pairs)


def cheb_nodes():
    return np.cos(np.pi * (2.0 * np.arange(8) + 1.0) / 16.0)


def lagrange_child(child_half):
    nodes = cheb_nodes()
    targets = (2.0 * child_half - 1.0) / 2.0 + nodes / 2.0
    result = np.ones((8, 8))
    for target in range(8):
        for factor in range(8):
            if factor != target:
                result[target, :] = (
                    result[target, :] * (targets - nodes[factor]) / (nodes[target] - nodes[factor])
                )
    return result


def kron_stack(along_second):
    matrices = []
    for child_half in range(2):
        lagrange = lagrange_child(child_half)
        if along_second:
            middle = np.kron(np.eye(8), lagrange)
        else:
            middle = np.kron(lagrange, np.eye(8))
        matrices.append(np.kron(np.eye(2), middle).T)
    return jnp.asarray(np.stack(matrices), dtype=jnp.float32)


def node_pattern(along_second):
    nodes = cheb_nodes()
    if along_second:
        layout = np.tile(nodes, 8)
    else:
        layout = np.repeat(nodes, 8)
    return jnp.asarray(layout, dtype=jnp.float32)


def rotate_apply(values, phases, kernel):
    angles = phases * TWO_PI
    cosine = jnp.cos(angles)
    sines = jnp.sin(angles)
    real_part = values[..., :64]
    imag_part = values[..., 64:]
    rotated = jnp.concatenate(
        [cosine * real_part - sines * imag_part, sines * real_part + cosine * imag_part], axis=-1
    )
    mapped = jnp.dot(
        rotated.reshape(-1, 128),
        kernel,
        precision=lax.Precision.HIGHEST,
        preferred_element_type=jnp.float32,
    )
    return mapped.reshape(values.shape)


def bend_factor(centre, across, offset):
    shifted = centre - offset
    return (
        offset
        * (centre + shifted)
        / (
            jnp.sqrt(centre * centre + across * across)
            + jnp.sqrt(shifted * shifted + across * across)
        )
    )


def path_bits(device_pos, level_num):
    result = jnp.int32(0)
    for shift in range(level_num):
        result = result + ((device_pos >> shift & 1) << level_num - 1 - shift)
    return result


def x_term(current, table_rows, level_num, path_value, box_pos, pick_half, n_gx):
    freq_boxes = current.shape[0]
    columns = current.shape[1]
    box_width = N / (MX * 2**level_num)
    kernels = kron_stack(False)
    pattern = node_pattern(False)
    centre = (
        (jnp.arange(freq_boxes) * 2**level_num + path_value).astype(jnp.float32) + 0.5
    ) * box_width - N / 2
    across = (jnp.arange(columns).astype(jnp.float32) + 0.5) * (N / MY) - N / 2
    offset = box_width / 4 * (1 - 2 * pick_half).astype(jnp.float32)
    bending = bend_factor(centre[:, None], across[None, :], offset)
    location = (box_pos.astype(jnp.float32) + 0.5 + 0.5 * pattern) * (2**level_num / n_gx)
    start_row = sum((n_gx >> shift for shift in range(level_num)))
    coef_row = lax.dynamic_index_in_dim(table_rows, start_row + box_pos, 0, keepdims=False)
    phases = location[None, None, :] * offset + coef_row[None, None, :] * bending[:, :, None]
    return rotate_apply(current, phases, kernels[box_pos % 2])


def y_term(current, table_rows, level_num, path_value, box_pos, pick_half, n_gy, m_start, n_gx):
    row_count = current.shape[0]
    freq_boxes = current.shape[1]
    box_width = N / (MY * 2**level_num)
    kernels = kron_stack(True)
    pattern = node_pattern(True)
    leading = ((m_start + jnp.arange(row_count)).astype(jnp.float32) + 0.5) * (
        N / (MX * n_gx)
    ) - N / 2
    centre = (
        (jnp.arange(freq_boxes) * 2**level_num + path_value).astype(jnp.float32) + 0.5
    ) * box_width - N / 2
    offset = box_width / 4 * (1 - 2 * pick_half).astype(jnp.float32)
    bending = bend_factor(centre[None, :], leading[:, None], offset)
    location = (box_pos.astype(jnp.float32) + 0.5 + 0.5 * pattern) * (2**level_num / n_gy)
    start_row = sum((n_gy >> shift for shift in range(level_num)))
    coef_row = lax.dynamic_index_in_dim(table_rows, start_row + box_pos, 0, keepdims=False)
    phases = location[None, None, :] * offset + coef_row[None, None, :] * bending[:, :, None]
    return rotate_apply(current, phases, kernels[box_pos % 2])


def on_device(weights, coef_first, coef_second):
    n_gx = lax.axis_size("gx")
    n_gy = lax.axis_size("gy")
    x_bits = n_gx.bit_length() - 1
    y_bits = n_gy.bit_length() - 1
    gx_index = lax.axis_index("gx")
    gy_index = lax.axis_index("gy")
    table_first = coef_first[0]
    current = weights[0, 0]
    per_block = MX // n_gx
    for level_num in range(x_bits):
        box_pos = gx_index >> level_num
        own_half = box_pos % 2
        path_value = path_bits(gx_index, level_num)
        partner = from_partner(current, "gx", level_num)
        current = x_term(
            current, table_first, level_num, path_value, box_pos, own_half, n_gx
        ) + x_term(partner, table_first, level_num, path_value, box_pos ^ 1, own_half, n_gx)
    blocks = current.reshape(n_gx, per_block, MY, 128)
    gathered = lax.all_to_all(blocks, "gx", split_axis=0, concat_axis=0, tiled=True)
    gathered = gathered.reshape((2,) * x_bits + (per_block, MY, 128))
    gathered = jnp.transpose(
        gathered, tuple(reversed(range(x_bits))) + tuple(range(x_bits, x_bits + 3))
    )
    gathered = gathered.reshape(n_gx, per_block, MY, 128)
    current = jnp.transpose(gathered, (1, 0, 2, 3)).reshape(MX, MY, 128)
    m_start = gx_index * MX
    for level_num in range(y_bits):
        box_pos = gy_index >> level_num
        own_half = box_pos % 2
        path_value = path_bits(gy_index, level_num)
        partner = from_partner(current, "gy", level_num)
        current = y_term(
            current, coef_second, level_num, path_value, box_pos, own_half, n_gy, m_start, n_gx
        ) + y_term(
            partner, coef_second, level_num, path_value, box_pos ^ 1, own_half, n_gy, m_start, n_gx
        )
    return current[None]


LANES = 128
AHEAD = 1
HOLD = 1
MESH = pl.DeviceIdType.MESH


def blocks_fit(n_gx, n_gy):
    per_gx = MX // n_gx
    if MX % n_gx or (per_gx * MY) % LANES or LANES % MY or n_gy % n_gx:
        return False
    return (per_gx * MY // LANES) % (n_gy // n_gx) == 0


def chebyshev_fit(func, degree):
    grid = 0.25 * (1 + np.cos(np.pi * (np.arange(400) + 0.5) / 400)) * 0.5
    series = np.polynomial.chebyshev.Chebyshev.fit(grid, func(grid), degree, domain=[0.0, 0.25])
    return [float(c) for c in series.convert(kind=np.polynomial.Polynomial).coef]


def horner(coefs, arg):
    result = coefs[-1]
    for coef in coefs[-2::-1]:
        result = result * arg + coef
    return result


COS_FIT = chebyshev_fit(lambda t: np.cos(np.pi * np.sqrt(t)), 5)
SIN_FIT = chebyshev_fit(lambda t: 2.0 * np.sinc(np.sqrt(t)) * np.pi, 5)
ROUNDER = 1.5 * 2.0**23


def cos_sin_turns(turns):
    part = turns - ((turns + ROUNDER) - ROUNDER)
    square = part * part
    cos_half = horner(COS_FIT, square)
    twice_sin_half = horner(SIN_FIT, square) * part
    return 1.0 - 0.5 * (twice_sin_half * twice_sin_half), twice_sin_half * cos_half


def merge(load, coef, bending, scale, box, store):
    nodes = cheb_nodes()
    lagrange = lagrange_child(0)
    plus = [[None] * 4, [None] * 4]
    minus = [[None] * 4, [None] * 4]
    bases = [scale * (2 * box + c + 0.5) for c in range(2)]
    for s in range(8):
        rotated = []
        for c in range(2):
            at = s if c == 0 else 7 - s
            turns = coef(c, at) * bending + (bases[c] + scale * float(0.5 * nodes[at]))
            cosine, sine = cos_sin_turns(turns)
            real, imag = load(c, 0, at), load(c, 1, at)
            rotated.append((cosine * real - sine * imag, sine * real + cosine * imag))
        for r in range(2):
            total = rotated[0][r] + rotated[1][r]
            apart = rotated[0][r] - rotated[1][r]
            for a in range(4):
                even = total * float(0.5 * (lagrange[a, s] + lagrange[7 - a, s]))
                odd = apart * float(0.5 * (lagrange[a, s] - lagrange[7 - a, s]))
                plus[r][a] = even if s == 0 else plus[r][a] + even
                minus[r][a] = odd if s == 0 else minus[r][a] + odd
    for r in range(2):
        for a in range(4):
            store(r, a, plus[r][a] + minus[r][a])
            store(r, 7 - a, plus[r][a] - minus[r][a])


def far_first(me, count, step):
    half = count // 2
    side = (me // half + 1 + step // half) % 2
    return side * half + (me % half + half // 2 + step) % half


def wait_bytes(ref, sem):
    pltpu.make_async_copy(ref, ref, sem).wait()


def butterfly_kernel(
    n_gx, n_gy, w_ref, cf_ref, cs_ref, o_ref,
    x_in, x_a, x_b, x_out, y_in, y_a, y_b, y_t, y_out, cx, cy,
    send_a, recv_a, send_b, recv_b, send_c, recv_c,
):
    gx = lax.axis_index("gx")
    gy = lax.axis_index("gy")
    x_bits = n_gx.bit_length() - 1
    y_bits = n_gy.bit_length() - 1
    per_gx = MX // n_gx
    rows = LANES // MY
    n_lb = per_gx // rows
    fan = n_gy // n_gx
    n_slot = n_lb // fan

    barrier = pltpu.get_barrier_semaphore()
    for step in range(1, n_gx):
        pl.semaphore_signal(
            barrier, inc=1, device_id=((gx + step) % n_gx, gy), device_id_type=MESH
        )
    for step in range(1, n_gy):
        pl.semaphore_signal(
            barrier, inc=1, device_id=(gx, (gy + step) % n_gy), device_id_type=MESH
        )
    pl.semaphore_wait(barrier, n_gx + n_gy - 2)

    def first_copy(lb, step):
        peer = (gx + step) % n_gx
        return pltpu.make_async_remote_copy(
            src_ref=w_ref.at[peer * n_lb + lb],
            dst_ref=x_in.at[gx, lb],
            send_sem=send_a.at[lb, step],
            recv_sem=recv_a.at[lb, gx],
            device_id=(peer, gy),
            device_id_type=MESH,
        )

    def first_start(lb):
        for step in range(1, n_gx):
            first_copy(lb, step).start()
        pltpu.make_async_copy(
            w_ref.at[gx * n_lb + lb], x_in.at[gx, lb], recv_a.at[lb, gx]
        ).start()

    for lb in range(min(AHEAD, n_lb)):
        first_start(lb)

    for source, spread in ((cf_ref, cx), (cs_ref, cy)):
        for row in range(source.shape[0]):
            line = jnp.broadcast_to(source[row].reshape(1, 64), (LANES, 64))
            spread[row] = line.T

    lane = lax.broadcasted_iota(jnp.int32, (8, LANES), 1)
    lane_m = lane // MY
    lane_b = lane % MY
    second = (lane_b.astype(jnp.float32) + 0.5) * (N / MY) - N / 2

    def first_block(lb):
        return gx * per_gx + lb * rows + lane_m

    def second_peer(lb, step):
        return (gy // fan + step) % n_gx * fan + lb % fan

    def second_copy(lb, peer, gets_local):
        z = peer // fan
        slot = lb // fan
        if gets_local:
            return pltpu.make_async_copy(
                x_out.at[lb, z], y_in.at[slot, gy], recv_b.at[slot, gy]
            )
        return pltpu.make_async_remote_copy(
            src_ref=x_out.at[lb, z],
            dst_ref=y_in.at[slot, gy],
            send_sem=send_b.at[lb, z],
            recv_sem=recv_b.at[slot, gy],
            device_id=(gx, peer),
            device_id_type=MESH,
        )

    def second_start(lb, peer):
        @pl.when(peer == gy)
        def _():
            second_copy(lb, peer, True).start()

        @pl.when(peer != gy)
        def _():
            second_copy(lb, peer, False).start()

    def x_block(lb, carry):
        for i in range(n_gx):
            wait_bytes(x_in.at[i, lb], recv_a.at[lb, i])

        @pl.when(lb + AHEAD < n_lb)
        def _():
            first_start(lb + AHEAD)

        def turn(i, carry):
            x_a[i] = x_in[i, lb].T
            return carry

        lax.fori_loop(0, n_gx, turn, 0)
        held, other = x_a, x_b
        for level in range(x_bits):
            halves = n_gx >> level + 1
            width = N / (MX * 2**level)
            start = sum(n_gx >> k for k in range(level))
            last = level == x_bits - 1
            target = x_out.at[lb] if last else other

            def unit(t, carry, held=held, target=target, halves=halves, width=width,
                     start=start, level=level, last=last):
                u = far_first(gy // fan, n_gx, t) if last else t
                box = u % halves
                path = u // halves
                sign = (1 - 2 * (path % 2)).astype(jnp.float32)
                centre = (
                    (first_block(lb) * 2**level + path // 2).astype(jnp.float32) + 0.5
                ) * width - N / 2
                bending = bend_factor(centre, second, sign * (width / 4))
                at = path // 2 * (2 * halves) + 2 * box

                def load(c, r, s):
                    return held[at + c, r * 64 + s * 8 : r * 64 + s * 8 + 8, :]

                def coef(c, s):
                    return cx[start + 2 * box + c, s * 8 : s * 8 + 8, :]

                def store(r, a, value):
                    target[u, r * 64 + a * 8 : r * 64 + a * 8 + 8, :] = value

                scale = sign * (width / 4 * 2**level / n_gx)
                merge(load, coef, bending, scale, box.astype(jnp.float32), store)
                if last:
                    second_start(lb, u * fan + lb % fan)
                return carry

            lax.fori_loop(0, n_gx, unit, 0)
            held, other = target, held

        return carry

    lax.fori_loop(0, n_lb, x_block, 0)

    def reverse(value):
        result = 0
        for shift in range(y_bits):
            result = result * 2 + value // 2**shift % 2
        return result

    def third_copy(slot, peer, gets_local):
        here = slot * fan + gy % fan
        place = o_ref.at[here, :, gy // fan]
        if gets_local:
            return pltpu.make_async_copy(y_out.at[slot, peer], place, recv_c.at[slot, gy])
        return pltpu.make_async_remote_copy(
            src_ref=y_out.at[slot, peer],
            dst_ref=place,
            send_sem=send_c.at[slot, peer],
            recv_sem=recv_c.at[slot, gy],
            device_id=(gx, peer),
            device_id_type=MESH,
        )

    def third_start(slot, peer):
        @pl.when(peer == gy)
        def _():
            third_copy(slot, peer, True).start()

        @pl.when(peer != gy)
        def _():
            third_copy(slot, peer, False).start()

    def y_block(slot, carry):
        lb = slot * fan + gy % fan
        leading = (
            (first_block(lb) * n_gx + gy // fan).astype(jnp.float32) + 0.5
        ) * (N / (MX * n_gx)) - N / 2
        for j in range(n_gy):
            wait_bytes(y_in.at[slot, j], recv_b.at[slot, j])

        def held_back(t, carry):
            third_start(slot - 1, (gy + n_gy // 2 + t) % n_gy)
            return carry

        @pl.when((slot >= 1) & (slot <= HOLD))
        def _():
            lax.fori_loop(0, n_gy, held_back, 0)

        held, target = y_in.at[slot], y_a
        for level in range(y_bits):
            halves = n_gy >> level + 1
            width = N / (MY * 2**level)
            start = sum(n_gy >> k for k in range(level))
            last = level == y_bits - 1

            def unit(t, carry, held=held, target=target, halves=halves, width=width,
                     start=start, level=level, last=last):
                if last:
                    peer = far_first(gy, n_gy, t)
                    u = reverse(peer)
                else:
                    u = t
                box = u % halves
                path = u // halves
                sign = (1 - 2 * (path % 2)).astype(jnp.float32)
                centre = (
                    (lane_b * 2**level + path // 2).astype(jnp.float32) + 0.5
                ) * width - N / 2
                bending = bend_factor(centre, leading, sign * (width / 4))
                at = path // 2 * (2 * halves) + 2 * box

                def load(c, r, s):
                    if level == 0:
                        return held[at + c, pl.ds(r * 64 + s, 8, stride=8), :]
                    return held[at + c, r * 64 + s * 8 : r * 64 + s * 8 + 8, :]

                def coef(c, s):
                    return cy[start + 2 * box + c, pl.ds(s, 8, stride=8), :]

                def store(r, b, value):
                    if last:
                        y_t[pl.ds(r * 64 + b, 8, stride=8), :] = value
                    else:
                        target[u, r * 64 + b * 8 : r * 64 + b * 8 + 8, :] = value

                scale = sign * (width / 4 * 2**level / n_gy)
                merge(load, coef, bending, scale, box.astype(jnp.float32), store)
                if last:
                    y_out[slot, peer] = y_t[...].T.reshape(rows, MY, LANES)

                    @pl.when(slot >= HOLD)
                    def _():
                        third_start(slot, peer)

                return carry

            lax.fori_loop(0, n_gy, unit, 0)
            held, target = target, (y_b if target is y_a else y_a)
        return carry

    lax.fori_loop(0, n_slot, y_block, 0)

    for lb in range(n_lb):
        for step in range(1, n_gx):
            first_copy(lb, step).wait_send()
        for step in range(n_gx):
            peer = second_peer(lb, step)

            @pl.when(peer != gy)
            def _():
                second_copy(lb, peer, False).wait_send()

    for slot in range(n_slot):
        for step in range(1, n_gy):
            third_copy(slot, (gy + step) % n_gy, False).wait_send()
        for j in range(n_gy):
            wait_bytes(o_ref.at[slot * fan + j % fan, :, j // fan], recv_c.at[slot, j])


def by_blocks(weights, coef_first, coef_second):
    n_gx = lax.axis_size("gx")
    n_gy = lax.axis_size("gy")
    per_gx = MX // n_gx
    rows = LANES // MY
    n_lb = per_gx // rows
    n_slot = n_lb // (n_gy // n_gx)
    block = (LANES, LANES)
    vmem = functools.partial(pltpu.VMEM, dtype=jnp.float32)
    dma = pltpu.SemaphoreType.DMA
    table_first = jnp.transpose(coef_first, (1, 0, 2))
    finished = pl.pallas_call(
        functools.partial(butterfly_kernel, n_gx, n_gy),
        out_shape=jax.ShapeDtypeStruct((n_lb, rows, n_gx, MY, LANES), jnp.float32),
        in_specs=[
            pl.BlockSpec(memory_space=pltpu.HBM),
            pl.BlockSpec(memory_space=pltpu.VMEM),
            pl.BlockSpec(memory_space=pltpu.VMEM),
        ],
        out_specs=pl.BlockSpec(memory_space=pl.ANY),
        scratch_shapes=[
            vmem((n_gx, n_lb) + block),
            vmem((n_gx,) + block),
            vmem((n_gx,) + block),
            vmem((n_lb, n_gx) + block),
            vmem((n_slot, n_gy) + block),
            vmem((n_gy,) + block),
            vmem((n_gy,) + block),
            vmem(block),
            vmem((n_slot, n_gy, rows, MY, LANES)),
            vmem((table_first.shape[0], 64, LANES)),
            vmem((coef_second.shape[0], 64, LANES)),
            dma((n_lb, n_gx)),
            dma((n_lb, n_gx)),
            dma((n_lb, n_gx)),
            dma((n_slot, n_gy)),
            dma((n_slot, n_gy)),
            dma((n_slot, n_gy)),
        ],
        compiler_params=pltpu.CompilerParams(
            collective_id=0, has_side_effects=True, vmem_limit_bytes=52 * 2**20
        ),
        name="butterfly",
    )(weights.reshape(n_gx * n_lb, LANES, LANES), table_first, coef_second)
    return finished.reshape(1, per_gx * n_gx, MY, LANES)


def solution(mesh):
    in_specs = (P("gx", "gy", None, None, None), P("gy", None, None), P())
    out_specs = P("gy", "gx", None, None)
    fits = blocks_fit(mesh.shape["gx"], mesh.shape["gy"])
    return jax.shard_map(
        by_blocks if fits else on_device,
        mesh=mesh,
        in_specs=in_specs,
        out_specs=out_specs,
        check_vma=False,
    )
```
